32 devices in a mesh: panel: 8 (over y, x, core), hist: 4 (over z).
Axes of the slice: x: 2, y: 2, z: 4, core: 2. Of those that a mesh axis runs over, the one named last changes fastest.
Arguments:
- excitation: bfloat16 [2, 32, 128, 128], P(None, 'panel'), may hold values from -8 to 8
- past: bfloat16 [16, 32, 128, 128], P('hist', 'panel'), may hold values from -6 to 6
- hist_tiles: bfloat16 [16, 32, 5, 128, 128], P('hist', 'panel'), may hold values from -0.078125 to 0.078125
- hist_src: int32 [16, 32, 5], P('hist', 'panel'), may hold values from -4 to 4, as said below
- hist_count: int32 [16, 32], P('hist', 'panel'), may hold values from 1 to 5, as said below
- near_tiles: bfloat16 [32, 3, 128, 128], P('panel'), may hold values from -0.5 to 4, as said below
Outputs:
- currents: bfloat16 [2, 32, 128, 128], P(None, 'panel', None, 'hist')
The draws below stay inside these ranges and needn't reach their ends.
Inputs may be any that keep to these rules, and one draw needn't show every extreme that they name: `hist_src`: the offsets within one shell and target block are distinct. `hist_count`: in every shell some block has all 5 slots live. The diagonal entries of every near_tiles[n, 1] lie between 2 and 4.
All inputs are finite; a program needn't handle non-finite values.
Results may differ from the reference program's by a relative error of at most 0.0054.
Values may be sent and summed in bfloat16 or wider, within the bound.
A program may use at most 64 MiB of HBM per device.

```python
import jax
import jax.numpy as jnp
from jax import lax

PANELS = 128
PORTS = 128
WIN = 4
TPB = 5
SWEEPS = 3
NB = 32
H = 16


def draw_hist_src(key, part):
    key = jax.random.fold_in(key, 11)
    spread = 2 * WIN + 1
    scores = jax.random.randint(key, (H, NB, spread), 0, 1 << 20) * spread + jnp.arange(spread, dtype=jnp.int32)
    order = jnp.argsort(scores, axis=-1, stable=True)
    return (order[:, :, :TPB] - WIN).astype(jnp.int32)


def draw_hist_count(key, part):
    key = jax.random.fold_in(key, 12)
    counts = jax.random.randint(key, (H, NB), 1, TPB + 1)
    shells = jnp.arange(H, dtype=jnp.int32)[:, None]
    blocks = jnp.arange(NB, dtype=jnp.int32)[None, :]
    return jnp.where(blocks == (shells * 7 + 3) % NB, TPB, counts).astype(jnp.int32)


def draw_near_tiles(key, part):
    key = jax.random.fold_in(key, 13)
    first_key, second_key = jax.random.split(key)
    scale = 1.0 / jnp.sqrt(jnp.float32(PANELS))
    offdiag = jax.random.normal(first_key, (NB, 3, PANELS, PANELS), jnp.float32) * scale
    offdiag = jnp.clip(offdiag, -0.5, 0.5)
    diagonal = jax.random.uniform(second_key, (NB, PANELS), jnp.float32, 2.0, 4.0)
    eye = jnp.eye(PANELS, dtype=jnp.float32)
    centre = offdiag[:, 1] * (1.0 - eye) + eye * diagonal[:, :, None]
    return offdiag.at[:, 1].set(centre).astype(jnp.bfloat16)


def block_levels(stream_key, dims, cuts, smallest, top_value):
    loudness, own = 1.0, jax.random.fold_in(stream_key, 6)
    for axis_at, shards_of in cuts:
        steps = jnp.exp(jax.random.uniform(jax.random.fold_in(own, axis_at), (shards_of,), jnp.float32, smallest / len(cuts), top_value / len(cuts)))
        loudness = loudness * jnp.repeat(steps, dims[axis_at] // shards_of).reshape([-1 if axis == axis_at else 1 for axis in range(len(dims))])
    return loudness


def noise(own_key, shape, width, limit, shards=(), held_as=jnp.bfloat16):
    result = jax.random.normal(own_key, shape, jnp.float32) * width
    if len(shards) > 0:
        result = block_levels(own_key, shape, shards, -0.22, 0.18) * result
    return jnp.clip(result, min=-limit, max=limit).astype(held_as)


def setup_inputs(seed: int = 0) -> dict:
    key_of = jax.random.split(jax.random.key(seed), 7)
    return {
        "excitation": noise(key_of[0], (2, NB, PANELS, PORTS), 3.0, 8.0, ((1, 8),)),
        "past": noise(key_of[1], (H, NB, PANELS, PORTS), 1.0, 6.0, ((0, 4), (1, 8))),
        "hist_tiles": noise(key_of[2], (H, NB, TPB, PANELS, PANELS), (PANELS * TPB * H // 2) ** -0.5, 0.078125, ((0, 4), (1, 8))),
        "hist_src": draw_hist_src(jax.random.fold_in(key_of[6], 71), 0),
        "hist_count": draw_hist_count(jax.random.fold_in(key_of[6], 71), 0),
        "near_tiles": draw_near_tiles(jax.random.fold_in(key_of[6], 71), 0),
    }


def history_field(history, hist_tiles, hist_src, hist_count):
    def one_shell(total, pieces):
        shell, tiles, source, count = pieces
        padded = jnp.pad(shell, ((WIN, WIN), (0, 0), (0, 0)))
        index = (jnp.arange(NB, dtype=jnp.int32)[:, None] + WIN + source).astype(jnp.int32)
        taken = padded[index].astype(jnp.float32)
        live = jnp.arange(TPB, dtype=jnp.int32)[None, :] < count[:, None]
        taken = jnp.where(live[:, :, None, None], taken, jnp.zeros((), jnp.float32))
        part = jnp.einsum('nsij,nsjp->nip', tiles.astype(jnp.float32), taken)
        return total + part, None

    start = jnp.zeros((NB, PANELS, PORTS), jnp.float32)
    total, _ = lax.scan(one_shell, start, (history, hist_tiles, hist_src, hist_count))
    return total


def jacobi(drive, near_tiles):
    diag = jnp.diagonal(near_tiles[:, 1], axis1=1, axis2=2).astype(jnp.float32)[:, :, None]
    state = drive / diag
    near32 = near_tiles.astype(jnp.float32)
    for sweep in range(SWEEPS - 1):
        rounded = state.astype(jnp.bfloat16).astype(jnp.float32)
        padded = jnp.pad(rounded, ((1, 1), (0, 0), (0, 0)))
        applied = jnp.einsum('nij,njp->nip', near32[:, 0], padded[:-2])
        applied = applied + jnp.einsum('nij,njp->nip', near32[:, 1], padded[1:-1])
        applied = applied + jnp.einsum('nij,njp->nip', near32[:, 2], padded[2:])
        state = state + (drive - applied) / diag
    return state.astype(jnp.bfloat16)


def reference(excitation, past, hist_tiles, hist_src, hist_count, near_tiles):
    field_one = history_field(past, hist_tiles, hist_src, hist_count)
    first = jacobi(excitation[0].astype(jnp.float32) - field_one, near_tiles)
    history = jnp.concatenate([first[None], past[:-1]], axis=0)
    field_two = history_field(history, hist_tiles, hist_src, hist_count)
    second = jacobi(excitation[1].astype(jnp.float32) - field_two, near_tiles)
    return jnp.stack([first, second], axis=0)
```

```python
import functools

import jax
import jax.numpy as jnp
from jax import lax
from jax.experimental import pallas as pl
from jax.experimental.pallas import tpu as pltpu
from jax.sharding import PartitionSpec as P

WIN = 4
MESH = pl.DeviceIdType.MESH
F32 = jnp.float32
BF16 = jnp.bfloat16
NT = (((1,), (1,)), ((), ()))


def kernel(
    panels_n, hist_n,
    exc_ref, past_ref, tiles_ref, src_hbm, count_hbm, near_ref, src_ref, count_ref,
    out_ref,
    c0, c1, c2, c3, cprev, tv, t0, ne, exv, acc, drive, rs_out, rs_in, rs_out2, rs_in2,
    xe, xe2, cu, srcv, countv, srcs, counts,
    past_s, past_r, zown_s, zown_r, cp_s, cp_r, t0_s, t0_r, ix_s, ix_r, ne_s, ne_r,
    rs_s, rs_r, rs2_s, rs2_r, xe_s, xe_r, xe2_s, xe2_r, cu_s, cu_r,
    lpast, ltile, lnear, lexc, lt0, lix,
):
    cs = (c0, c1, c2, c3)
    shells, blocks, slots = tiles_ref.shape[:3]
    size = tiles_ref.shape[3]
    share = out_ref.shape[2]
    me = lax.axis_index("panel")
    zed = lax.axis_index("hist")
    has_l, has_r = me > 0, me < panels_n - 1
    has_d, has_u = zed > 0, zed < hist_n - 1
    none = blocks + 2 * WIN

    def when(condition, action):
        pl.when(condition)(action)

    local_past = [
        pltpu.make_async_copy(past_ref.at[k], cs[k].at[pl.ds(WIN, blocks)], lpast.at[k])
        for k in range(shells)
    ]
    local_tile = [
        pltpu.make_async_copy(tiles_ref.at[k], tv.at[k], ltile.at[k]) for k in range(shells)
    ]
    local_near = pltpu.make_async_copy(near_ref, ne.at[pl.ds(1, blocks)], lnear)
    local_exc = pltpu.make_async_copy(exc_ref, exv, lexc)
    local_t0 = pltpu.make_async_copy(tiles_ref.at[0], t0, lt0)
    local_ix = [
        pltpu.make_async_copy(src_hbm.at[0], srcv, lix.at[0]),
        pltpu.make_async_copy(count_hbm, countv, lix.at[1]),
    ]

    def pair(send, recv, out_right, in_left, out_left, in_right):
        right = pltpu.make_async_remote_copy(
            src_ref=out_right, dst_ref=in_left, send_sem=send.at[0], recv_sem=recv.at[0],
            device_id={"panel": jnp.minimum(me + 1, panels_n - 1)}, device_id_type=MESH,
        )
        left = pltpu.make_async_remote_copy(
            src_ref=out_left, dst_ref=in_right, send_sem=send.at[1], recv_sem=recv.at[1],
            device_id={"panel": jnp.maximum(me - 1, 0)}, device_id_type=MESH,
        )
        return right, left

    def pair_start(p):
        when(has_r, p[0].start)
        when(has_l, p[1].start)

    def pair_recv(p):
        when(has_l, p[0].wait_recv)
        when(has_r, p[1].wait_recv)

    def pair_send(p):
        when(has_r, p[0].wait_send)
        when(has_l, p[1].wait_send)

    low, high = pl.ds(0, WIN), pl.ds(WIN + blocks, WIN)
    first, last = pl.ds(WIN, WIN), pl.ds(blocks, WIN)
    past_pairs = [
        pair(
            past_s.at[k], past_r.at[k],
            past_ref.at[k, pl.ds(blocks - WIN, WIN)], cs[k].at[low],
            past_ref.at[k, pl.ds(0, WIN)], cs[k].at[high],
        )
        for k in range(shells)
    ]
    cp_pair = pair(cp_s, cp_r, cprev.at[last], cprev.at[low], cprev.at[first], cprev.at[high])
    near_pair = pair(
        ne_s, ne_r, near_ref.at[blocks - 1], ne.at[0], near_ref.at[0], ne.at[blocks + 1]
    )
    xe_out = (pl.ds(blocks, 2), pl.ds(0, 2), pl.ds(2, 2), pl.ds(blocks + 2, 2))
    xe_pair = pair(xe_s, xe_r, *[xe.at[w] for w in xe_out])
    xe2_pair = pair(xe2_s, xe2_r, *[xe2.at[w] for w in xe_out])
    cu_pair = pair(cu_s, cu_r, cu.at[last], cu.at[low], cu.at[first], cu.at[high])

    above = {"hist": jnp.minimum(zed + 1, hist_n - 1)}
    zown = pltpu.make_async_remote_copy(
        src_ref=past_ref.at[shells - 1], dst_ref=cprev.at[pl.ds(WIN, blocks)],
        send_sem=zown_s, recv_sem=zown_r, device_id=above, device_id_type=MESH,
    )

    def t0_copy(chunk, source):
        return pltpu.make_async_remote_copy(
            src_ref=source, dst_ref=t0.at[chunk], send_sem=t0_s.at[chunk],
            recv_sem=t0_r.at[chunk], device_id=above, device_id_type=MESH,
        )

    def t0_forward(chunk):
        def go():
            copy = t0_copy(chunk, t0.at[chunk])
            copy.wait_recv()
            when(has_u, copy.start)
        return go

    def t0_point(where):
        for chunk in range(blocks):
            for at in range(1, 4):
                when_at = {1: 1 + chunk, 2: 3 + chunk - (chunk > 1), 3: 5}[at]
                when_at = min(when_at, 5)
                if when_at == where:
                    when((zed == at) if at < 3 else (zed >= at), t0_forward(chunk))

    ix_copies = []
    for other in range(1, hist_n):
        ix_copies.append([
            pltpu.make_async_remote_copy(
                src_ref=source, dst_ref=target, send_sem=ix_s.at[other - 1, j],
                recv_sem=ix_r.at[j], device_id={"hist": other}, device_id_type=MESH,
            )
            for j, (source, target) in enumerate(((src_hbm.at[0], srcv), (count_hbm, countv)))
        ])

    def reduce_copies(send, recv, out, into):
        copies = []
        for step in range(1, hist_n):
            other = lax.rem(zed + step, hist_n)
            copies.append(pltpu.make_async_remote_copy(
                src_ref=out.at[other], dst_ref=into.at[step - 1],
                send_sem=send.at[step - 1], recv_sem=recv.at[step - 1],
                device_id={"hist": other}, device_id_type=MESH,
            ))
        return copies

    rs_copies = reduce_copies(rs_s, rs_r, rs_out, rs_in)
    rs2_copies = reduce_copies(rs2_s, rs2_r, rs_out2, rs_in2)

    for copy in local_past + [local_near, local_exc] + local_tile:
        copy.start()

    def at_zero():
        local_t0.start()
        for copy in local_ix:
            copy.start()
    when(zed == 0, at_zero)

    barrier = pltpu.get_barrier_semaphore()

    def greet(device):
        return lambda: pl.semaphore_signal(
            barrier, inc=1, device_id=device, device_id_type=MESH
        )
    when(has_r, greet({"panel": jnp.minimum(me + 1, panels_n - 1)}))
    when(has_l, greet({"panel": jnp.maximum(me - 1, 0)}))
    for step in range(1, hist_n):
        greet({"hist": lax.rem(zed + step, hist_n)})()
    for c in cs + (cprev,):
        c[none] = jnp.zeros((size, size), BF16)
    cu[none] = jnp.zeros((share, size), BF16)
    pl.semaphore_wait(
        barrier, hist_n - 1 + has_r.astype(jnp.int32) + has_l.astype(jnp.int32)
    )

    for p in past_pairs:
        pair_start(p)

    def spread():
        for copies in ix_copies:
            for copy in copies:
                copy.start()
        for chunk in range(blocks):
            t0_copy(chunk, tiles_ref.at[0, chunk]).start()
    when(zed == 0, spread)
    when(has_u, zown.start)

    local_exc.wait()
    for t in range(2):
        for n in range(blocks):
            drive[t, n] = exv[t, n].astype(F32).T
    local_near.wait()
    eye = lax.broadcasted_iota(jnp.int32, (size, size), 0) == lax.broadcasted_iota(
        jnp.int32, (size, size), 1
    )

    def diagonal(tile):
        return jnp.sum(jnp.where(eye, tile.astype(F32), 0.0), axis=0, keepdims=True)

    diag = {e: diagonal(ne[e, 1]) for e in range(1, blocks + 1)}

    def place(source, count, n, s):
        block = me * blocks + n + source
        live = (s < count) & (block >= 0) & (block < panels_n * blocks)
        return jnp.where(live, n + source + WIN, none)

    def tile_row(ref, n):
        return jnp.concatenate([ref[n, s] for s in range(slots)], axis=1)

    for k in range(shells):
        local_past[k].wait()
        local_tile[k].wait()
        pair_recv(past_pairs[k])
        if k == 2:
            pair_start(near_pair)
        for n in range(blocks):
            at = [place(src_ref[k, n, s], count_ref[k, n], n, s) for s in range(slots)]
            left = tile_row(tv.at[k], n)
            right = jnp.concatenate([cs[k][i] for i in at], axis=0)
            if k > 0:
                older = jnp.concatenate([cs[k - 1][i] for i in at], axis=0)
                right = jnp.concatenate([right, older], axis=1)
            part = jnp.dot(left, right, preferred_element_type=F32)
            if k == 0:
                acc[n, :, pl.ds(0, size)] = part
            elif k == 1:
                acc[n, :, pl.ds(0, size)] += part[:, :size]
                acc[n, :, pl.ds(size, size)] = part[:, size:]
            else:
                acc[n] += part
        t0_point(k)

    mine = pl.ds(pl.multiple_of(zed * share, share), share)

    for n in range(blocks):
        field = acc[n, :, pl.ds(0, size)].T
        drive[0, n] -= field
        rs_out[:, n] = field.reshape(hist_n, share, size).astype(BF16)
    for copy in rs_copies:
        copy.start()

    def pass_on():
        zown.wait_recv()
        pair_start(cp_pair)
    when(has_d, pass_on)
    for copy in rs_copies:
        copy.wait_recv()

    def driven(t, n, into):
        g = drive[t, n, mine]
        for step in range(hist_n - 1):
            g = g - into[step, n].astype(F32)
        return g

    def begin(g, states, copy_pair):
        x = [g[n] / diag[n + 1] for n in range(blocks)]
        for n in range(blocks):
            states[n + 2] = x[n].astype(BF16)
        pair_start(copy_pair)
        return x

    g = [driven(0, n, rs_in) for n in range(blocks)]
    x = begin(g, xe, xe_pair)
    t0_point(4)

    def older_shell():
        pair_recv(cp_pair)
        for n in range(blocks):
            at = [place(src_ref[0, n, s], count_ref[0, n], n, s) for s in range(slots)]
            right = jnp.concatenate([cprev[i] for i in at], axis=0)
            acc[n, :, pl.ds(size, size)] += jnp.dot(
                tile_row(tv.at[0], n), right, preferred_element_type=F32
            )
    when(has_d, older_shell)
    for n in range(blocks):
        field = acc[n, :, pl.ds(size, size)].T
        drive[1, n] -= field
        rs_out2[:, n] = field.reshape(hist_n, share, size).astype(BF16)
    for copy in rs2_copies:
        copy.start()
    pair_recv(near_pair)
    for e in (0, blocks + 1):
        diag[e] = diagonal(ne[e, 1])

    def applied(states, e):
        tiles = jnp.concatenate([ne[e, j] for j in range(3)], axis=1)
        return lax.dot_general(
            jnp.concatenate(states, axis=1), tiles, NT, preferred_element_type=F32
        )

    def sweeps(g, x, states, copy_pair):
        pair_recv(copy_pair)
        empty = jnp.zeros((share, size), BF16)
        held = [states[j] for j in range(blocks + 4)]
        for j in range(2):
            held[j] = jnp.where(has_l, held[j], empty)
            held[blocks + 2 + j] = jnp.where(has_r, held[blocks + 2 + j], empty)
        new = []
        for e in range(blocks + 2):
            by = applied(held[e : e + 3], e)
            if 0 < e <= blocks:
                x[e - 1] = x[e - 1] + (g[e - 1] - by) / diag[e]
                new.append(x[e - 1].astype(BF16))
            else:
                start = held[e + 1].astype(F32)
                value = (start + (start - by / diag[e])).astype(BF16)
                new.append(jnp.where(has_l if e == 0 else has_r, value, empty))
        return [
            (x[n] + (g[n] - applied(new[n : n + 3], n + 1)) / diag[n + 1]).astype(BF16)
            for n in range(blocks)
        ]

    now = sweeps(g, x, xe, xe_pair)
    for n in range(blocks):
        cu[WIN + n] = now[n]
    pair_start(cu_pair)
    for n in range(blocks):
        out_ref[0, n] = now[n]
    t0_point(5)

    def here():
        local_t0.wait()
        for copy in local_ix:
            copy.wait()

    def there():
        for copy in ix_copies[0]:
            copy.wait_recv()
    when(zed == 0, here)
    when(zed > 0, there)
    to_scalar = [
        pltpu.make_async_copy(srcv, srcs, lix.at[2]),
        pltpu.make_async_copy(countv, counts, lix.at[3]),
    ]
    for copy in to_scalar:
        copy.start()
    for copy in rs2_copies:
        copy.wait_recv()
    g = [driven(1, n, rs_in2) for n in range(blocks)]
    for copy in to_scalar:
        copy.wait()
    pair_recv(cu_pair)
    for n in range(blocks):
        at = [place(srcs[n, s], counts[0, n], n, s) for s in range(slots)]
        left = jnp.concatenate([cu[i] for i in at], axis=1)
        g[n] = g[n] - lax.dot_general(
            left, tile_row(t0, n), NT, preferred_element_type=F32
        )
    x = begin(g, xe2, xe2_pair)
    now = sweeps(g, x, xe2, xe2_pair)
    for n in range(blocks):
        out_ref[1, n] = now[n]

    for p in past_pairs + [near_pair, xe_pair, xe2_pair, cu_pair]:
        pair_send(p)
    when(has_d, lambda: pair_send(cp_pair))
    for copy in rs_copies + rs2_copies:
        copy.wait_send()
    when(has_u, zown.wait_send)

    def t0_sent():
        for chunk in range(blocks):
            t0_copy(chunk, t0.at[chunk]).wait_send()
    when(has_u, t0_sent)

    def ix_sent():
        for copies in ix_copies:
            for copy in copies:
                copy.wait_send()
    when(zed == 0, ix_sent)


def shards(panels_n, hist_n, excitation, past, hist_tiles, hist_src, hist_count, near_tiles):
    shells, blocks, slots, size = hist_tiles.shape[:4]
    ports = past.shape[3]
    share = ports // hist_n
    any_space = pl.BlockSpec(memory_space=pl.ANY)
    scalar = pl.BlockSpec(memory_space=pltpu.SMEM)
    span = blocks + 2 * WIN + 1
    dma = pltpu.SemaphoreType.DMA
    vmem = pltpu.VMEM
    out = pl.pallas_call(
        functools.partial(kernel, panels_n, hist_n),
        out_shape=jax.ShapeDtypeStruct((2, blocks, share, size), BF16),
        in_specs=[any_space] * 6 + [scalar] * 2,
        out_specs=pl.BlockSpec(memory_space=pltpu.VMEM),
        scratch_shapes=[vmem((span, size, ports), BF16)] * 5
        + [
            vmem((shells, blocks, slots, size, size), BF16),
            vmem((blocks, slots, size, size), BF16),
            vmem((blocks + 2, 3, size, size), BF16),
            vmem((2, blocks, size, ports), BF16),
            vmem((blocks, size, 2 * ports), F32),
            vmem((2, blocks, ports, size), F32),
        ]
        + [
            vmem((hist_n, blocks, share, size), BF16),
            vmem((hist_n - 1, blocks, share, size), BF16),
        ] * 2
        + [
            vmem((blocks + 4, share, size), BF16),
            vmem((blocks + 4, share, size), BF16),
            vmem((span, share, size), BF16),
            vmem((blocks, slots), jnp.int32),
            vmem((shells, blocks), jnp.int32),
            pltpu.SMEM((blocks, slots), jnp.int32),
            pltpu.SMEM((shells, blocks), jnp.int32),
            dma((shells, 2)), dma((shells, 2)),
            dma, dma,
            dma((2,)), dma((2,)),
            dma((blocks,)), dma((blocks,)),
            dma((hist_n - 1, 2)), dma((2,)),
            dma((2,)), dma((2,)),
            dma((hist_n - 1,)), dma((hist_n - 1,)),
            dma((hist_n - 1,)), dma((hist_n - 1,)),
            dma((2,)), dma((2,)), dma((2,)), dma((2,)), dma((2,)), dma((2,)),
            dma((shells,)), dma((shells,)), dma, dma, dma, dma((4,)),
        ],
        compiler_params=pltpu.CompilerParams(
            collective_id=0, has_side_effects=True, vmem_limit_bytes=40 * 1024 * 1024
        ),
    )(excitation, past, hist_tiles, hist_src, hist_count, near_tiles, hist_src, hist_count)
    return jnp.swapaxes(out, 2, 3)


def solution(mesh):
    return jax.shard_map(
        functools.partial(shards, mesh.shape["panel"], mesh.shape["hist"]),
        mesh=mesh,
        in_specs=(
            P(None, "panel", None, None),
            P("hist", "panel", None, None),
            P("hist", "panel", None, None, None),
            P("hist", "panel", None),
            P("hist", "panel"),
            P("panel", None, None, None),
        ),
        out_specs=P(None, "panel", None, "hist"),
        check_vma=False,
    )
```

```python
import functools

import jax
import jax.numpy as jnp
from jax import lax
from jax.experimental import pallas as pl
from jax.experimental.pallas import tpu as pltpu
from jax.sharding import PartitionSpec as P

WIN = 4
MESH = pl.DeviceIdType.MESH
F32 = jnp.float32
BF16 = jnp.bfloat16
NT = (((1,), (1,)), ((), ()))


def kernel(
    panels_n, hist_n,
    exc_ref, past_ref, tiles_ref, src_hbm, count_hbm, near_ref, src_ref, count_ref,
    out_ref,
    c0, c1, c2, c3, cprev, tv, t0, ne, exv, acc, drive, rs_out, rs_in, rs_out2, rs_in2,
    xe, xe2, cu, srcv, countv, srcs, counts,
    past_s, past_r, zown_s, zown_r, cp_s, cp_r, t0_s, t0_r, ix_s, ix_r, ne_s, ne_r,
    rs_s, rs_r, rs2_s, rs2_r, xe_s, xe_r, xe2_s, xe2_r, cu_s, cu_r,
    lpast, ltile, lnear, lexc, lt0, lix,
):
    cs = (c0, c1, c2, c3)
    shells, blocks, slots = tiles_ref.shape[:3]
    size = tiles_ref.shape[3]
    share = out_ref.shape[2]
    me = lax.axis_index("panel")
    zed = lax.axis_index("hist")
    has_l, has_r = me > 0, me < panels_n - 1
    has_d, has_u = zed > 0, zed < hist_n - 1
    none = blocks + 2 * WIN

    def when(condition, action):
        pl.when(condition)(action)

    local_past = [
        pltpu.make_async_copy(past_ref.at[k], cs[k].at[pl.ds(WIN, blocks)], lpast.at[k])
        for k in range(shells)
    ]
    local_tile = [
        pltpu.make_async_copy(tiles_ref.at[k], tv.at[k], ltile.at[k]) for k in range(shells)
    ]
    local_near = pltpu.make_async_copy(near_ref, ne.at[pl.ds(1, blocks)], lnear)
    local_exc = pltpu.make_async_copy(exc_ref, exv, lexc)
    local_t0 = pltpu.make_async_copy(tiles_ref.at[0], t0, lt0)
    local_ix = [
        pltpu.make_async_copy(src_hbm.at[0], srcv, lix.at[0]),
        pltpu.make_async_copy(count_hbm, countv, lix.at[1]),
    ]

    def pair(send, recv, out_right, in_left, out_left, in_right):
        right = pltpu.make_async_remote_copy(
            src_ref=out_right, dst_ref=in_left, send_sem=send.at[0], recv_sem=recv.at[0],
            device_id={"panel": jnp.minimum(me + 1, panels_n - 1)}, device_id_type=MESH,
        )
        left = pltpu.make_async_remote_copy(
            src_ref=out_left, dst_ref=in_right, send_sem=send.at[1], recv_sem=recv.at[1],
            device_id={"panel": jnp.maximum(me - 1, 0)}, device_id_type=MESH,
        )
        return right, left

    def pair_start(p):
        when(has_r, p[0].start)
        when(has_l, p[1].start)

    def pair_recv(p):
        when(has_l, p[0].wait_recv)
        when(has_r, p[1].wait_recv)

    def pair_send(p):
        when(has_r, p[0].wait_send)
        when(has_l, p[1].wait_send)

    low, high = pl.ds(0, WIN), pl.ds(WIN + blocks, WIN)
    first, last = pl.ds(WIN, WIN), pl.ds(blocks, WIN)
    past_pairs = [
        pair(
            past_s.at[k], past_r.at[k],
            past_ref.at[k, pl.ds(blocks - WIN, WIN)], cs[k].at[low],
            past_ref.at[k, pl.ds(0, WIN)], cs[k].at[high],
        )
        for k in range(shells)
    ]
    cp_pair = pair(cp_s, cp_r, cprev.at[last], cprev.at[low], cprev.at[first], cprev.at[high])
    near_pair = pair(
        ne_s, ne_r, near_ref.at[blocks - 1], ne.at[0], near_ref.at[0], ne.at[blocks + 1]
    )
    xe_out = (pl.ds(blocks, 2), pl.ds(0, 2), pl.ds(2, 2), pl.ds(blocks + 2, 2))
    xe_pair = pair(xe_s, xe_r, *[xe.at[w] for w in xe_out])
    xe2_pair = pair(xe2_s, xe2_r, *[xe2.at[w] for w in xe_out])
    cu_pair = pair(cu_s, cu_r, cu.at[last], cu.at[low], cu.at[first], cu.at[high])

    above = {"hist": jnp.minimum(zed + 1, hist_n - 1)}
    zown = pltpu.make_async_remote_copy(
        src_ref=past_ref.at[shells - 1], dst_ref=cprev.at[pl.ds(WIN, blocks)],
        send_sem=zown_s, recv_sem=zown_r, device_id=above, device_id_type=MESH,
    )

    def t0_copy(chunk, source):
        return pltpu.make_async_remote_copy(
            src_ref=source, dst_ref=t0.at[chunk], send_sem=t0_s.at[chunk],
            recv_sem=t0_r.at[chunk], device_id=above, device_id_type=MESH,
        )

    def t0_forward(chunk):
        def go():
            copy = t0_copy(chunk, t0.at[chunk])
            copy.wait_recv()
            copy.start()
        return go

    def t0_point(where):
        for chunk in range(blocks):
            if where == (-1 if chunk < blocks - 1 else 0):
                when((zed == 1) & has_u, t0_forward(chunk))
            if where == (-1, 0, 3, 4)[min(chunk, 3)]:
                when((zed == 2) & has_u, t0_forward(chunk))
            if where == 6:
                when((zed > 2) & has_u, t0_forward(chunk))

    ix_copies = []
    for other in range(1, hist_n):
        ix_copies.append([
            pltpu.make_async_remote_copy(
                src_ref=source, dst_ref=target, send_sem=ix_s.at[other - 1, j],
                recv_sem=ix_r.at[j], device_id={"hist": other}, device_id_type=MESH,
            )
            for j, (source, target) in enumerate(((src_hbm.at[0], srcv), (count_hbm, countv)))
        ])

    def reduce_copies(send, recv, out, into):
        copies = []
        for step in range(1, hist_n):
            other = lax.rem(zed + step, hist_n)
            copies.append(pltpu.make_async_remote_copy(
                src_ref=out.at[other], dst_ref=into.at[step - 1],
                send_sem=send.at[step - 1], recv_sem=recv.at[step - 1],
                device_id={"hist": other}, device_id_type=MESH,
            ))
        return copies

    rs_copies = reduce_copies(rs_s, rs_r, rs_out, rs_in)
    rs2_copies = reduce_copies(rs2_s, rs2_r, rs_out2, rs_in2)

    for copy in local_past + [local_near, local_exc] + local_tile:
        copy.start()

    def at_zero():
        local_t0.start()
        for copy in local_ix:
            copy.start()
    when(zed == 0, at_zero)

    barrier = pltpu.get_barrier_semaphore()

    def greet(device):
        return lambda: pl.semaphore_signal(
            barrier, inc=1, device_id=device, device_id_type=MESH
        )
    when(has_r, greet({"panel": jnp.minimum(me + 1, panels_n - 1)}))
    when(has_l, greet({"panel": jnp.maximum(me - 1, 0)}))
    for step in range(1, hist_n):
        greet({"hist": lax.rem(zed + step, hist_n)})()
    for c in cs + (cprev,):
        c[none] = jnp.zeros((size, size), BF16)
    cu[none] = jnp.zeros((share, size), BF16)
    pl.semaphore_wait(
        barrier, hist_n - 1 + has_r.astype(jnp.int32) + has_l.astype(jnp.int32)
    )

    for p in past_pairs:
        pair_start(p)

    def spread():
        for copies in ix_copies:
            for copy in copies:
                copy.start()
        for chunk in range(blocks):
            t0_copy(chunk, tiles_ref.at[0, chunk]).start()
    when(zed == 0, spread)
    when(has_u, zown.start)

    local_exc.wait()
    for t in range(2):
        for n in range(blocks):
            drive[t, n] = exv[t, n].astype(F32).T
    local_near.wait()
    eye = lax.broadcasted_iota(jnp.int32, (size, size), 0) == lax.broadcasted_iota(
        jnp.int32, (size, size), 1
    )

    def diagonal(tile):
        return jnp.sum(jnp.where(eye, tile.astype(F32), 0.0), axis=0, keepdims=True)

    diag = {e: diagonal(ne[e, 1]) for e in range(1, blocks + 1)}

    def place(source, count, n, s):
        block = me * blocks + n + source
        live = (s < count) & (block >= 0) & (block < panels_n * blocks)
        return jnp.where(live, n + source + WIN, none)

    def tile_row(ref, n):
        return jnp.concatenate([ref[n, s] for s in range(slots)], axis=1)

    t0_point(-1)
    for k in range(shells):
        local_past[k].wait()
        local_tile[k].wait()
        pair_recv(past_pairs[k])
        if k == 2:
            pair_start(near_pair)
        for n in range(blocks):
            at = [place(src_ref[k, n, s], count_ref[k, n], n, s) for s in range(slots)]
            left = tile_row(tv.at[k], n)
            right = jnp.concatenate([cs[k][i] for i in at], axis=0)
            if k > 0:
                older = jnp.concatenate([cs[k - 1][i] for i in at], axis=0)
                right = jnp.concatenate([right, older], axis=1)
            part = jnp.dot(left, right, preferred_element_type=F32)
            if k == 0:
                acc[n, :, pl.ds(0, size)] = part
            elif k == 1:
                acc[n, :, pl.ds(0, size)] += part[:, :size]
                acc[n, :, pl.ds(size, size)] = part[:, size:]
            else:
                acc[n] += part
        t0_point(k)

    mine = pl.ds(pl.multiple_of(zed * share, share), share)

    for n in range(blocks):
        field = acc[n, :, pl.ds(0, size)].T
        drive[0, n] -= field
        rs_out[:, n] = field.reshape(hist_n, share, size).astype(BF16)
    for copy in rs_copies:
        copy.start()

    def pass_on():
        zown.wait_recv()
        pair_start(cp_pair)
    when(has_d, pass_on)
    t0_point(4)
    for copy in rs_copies:
        copy.wait_recv()

    def driven(t, n, into):
        g = drive[t, n, mine]
        for step in range(hist_n - 1):
            g = g - into[step, n].astype(F32)
        return g

    def begin(g, states, copy_pair):
        x = [g[n] / diag[n + 1] for n in range(blocks)]
        for n in range(blocks):
            states[n + 2] = x[n].astype(BF16)
        pair_start(copy_pair)
        return x

    g = [driven(0, n, rs_in) for n in range(blocks)]
    x = begin(g, xe, xe_pair)
    t0_point(5)

    def older_shell():
        pair_recv(cp_pair)
        for n in range(blocks):
            at = [place(src_ref[0, n, s], count_ref[0, n], n, s) for s in range(slots)]
            right = jnp.concatenate([cprev[i] for i in at], axis=0)
            acc[n, :, pl.ds(size, size)] += jnp.dot(
                tile_row(tv.at[0], n), right, preferred_element_type=F32
            )
    when(has_d, older_shell)
    for n in range(blocks):
        field = acc[n, :, pl.ds(size, size)].T
        drive[1, n] -= field
        rs_out2[:, n] = field.reshape(hist_n, share, size).astype(BF16)
    for copy in rs2_copies:
        copy.start()
    t0_point(6)
    pair_recv(near_pair)
    for e in (0, blocks + 1):
        diag[e] = diagonal(ne[e, 1])

    def applied(states, e):
        tiles = jnp.concatenate([ne[e, j] for j in range(3)], axis=1)
        return lax.dot_general(
            jnp.concatenate(states, axis=1), tiles, NT, preferred_element_type=F32
        )

    def sweeps(g, x, states, copy_pair):
        pair_recv(copy_pair)
        empty = jnp.zeros((share, size), BF16)
        held = [states[j] for j in range(blocks + 4)]
        for j in range(2):
            held[j] = jnp.where(has_l, held[j], empty)
            held[blocks + 2 + j] = jnp.where(has_r, held[blocks + 2 + j], empty)
        new = []
        for e in range(blocks + 2):
            by = applied(held[e : e + 3], e)
            if 0 < e <= blocks:
                x[e - 1] = x[e - 1] + (g[e - 1] - by) / diag[e]
                new.append(x[e - 1].astype(BF16))
            else:
                start = held[e + 1].astype(F32)
                value = (start + (start - by / diag[e])).astype(BF16)
                new.append(jnp.where(has_l if e == 0 else has_r, value, empty))
        return [
            (x[n] + (g[n] - applied(new[n : n + 3], n + 1)) / diag[n + 1]).astype(BF16)
            for n in range(blocks)
        ]

    now = sweeps(g, x, xe, xe_pair)
    for n in range(blocks):
        cu[WIN + n] = now[n]
    pair_start(cu_pair)
    for n in range(blocks):
        out_ref[0, n] = now[n]

    def here():
        local_t0.wait()
        for copy in local_ix:
            copy.wait()

    def there():
        for copy in ix_copies[0]:
            copy.wait_recv()

        def parts():
            for chunk in range(blocks):
                t0_copy(chunk, t0.at[chunk]).wait_recv()
        when(zed == hist_n - 1, parts)
    when(zed == 0, here)
    when(zed > 0, there)
    to_scalar = [
        pltpu.make_async_copy(srcv, srcs, lix.at[2]),
        pltpu.make_async_copy(countv, counts, lix.at[3]),
    ]
    for copy in to_scalar:
        copy.start()
    for copy in rs2_copies:
        copy.wait_recv()
    g = [driven(1, n, rs_in2) for n in range(blocks)]
    for copy in to_scalar:
        copy.wait()
    pair_recv(cu_pair)
    for n in range(blocks):
        at = [place(srcs[n, s], counts[0, n], n, s) for s in range(slots)]
        left = jnp.concatenate([cu[i] for i in at], axis=1)
        g[n] = g[n] - lax.dot_general(
            left, tile_row(t0, n), NT, preferred_element_type=F32
        )
    x = begin(g, xe2, xe2_pair)
    now = sweeps(g, x, xe2, xe2_pair)
    for n in range(blocks):
        out_ref[1, n] = now[n]

    for p in past_pairs + [near_pair, xe_pair, xe2_pair, cu_pair]:
        pair_send(p)
    when(has_d, lambda: pair_send(cp_pair))
    for copy in rs_copies + rs2_copies:
        copy.wait_send()
    when(has_u, zown.wait_send)

    def t0_sent():
        for chunk in range(blocks):
            t0_copy(chunk, t0.at[chunk]).wait_send()
    when(has_u, t0_sent)

    def ix_sent():
        for copies in ix_copies:
            for copy in copies:
                copy.wait_send()
    when(zed == 0, ix_sent)


def shards(panels_n, hist_n, excitation, past, hist_tiles, hist_src, hist_count, near_tiles):
    shells, blocks, slots, size = hist_tiles.shape[:4]
    ports = past.shape[3]
    share = ports // hist_n
    any_space = pl.BlockSpec(memory_space=pltpu.HBM)
    scalar = pl.BlockSpec(memory_space=pltpu.SMEM)
    span = blocks + 2 * WIN + 1
    dma = pltpu.SemaphoreType.DMA
    vmem = pltpu.VMEM
    out = pl.pallas_call(
        functools.partial(kernel, panels_n, hist_n),
        out_shape=jax.ShapeDtypeStruct((2, blocks, share, size), BF16),
        in_specs=[any_space] * 6 + [scalar] * 2,
        out_specs=pl.BlockSpec(memory_space=pltpu.VMEM),
        scratch_shapes=[vmem((span, size, ports), BF16)] * 5
        + [
            vmem((shells, blocks, slots, size, size), BF16),
            vmem((blocks, slots, size, size), BF16),
            vmem((blocks + 2, 3, size, size), BF16),
            vmem((2, blocks, size, ports), BF16),
            vmem((blocks, size, 2 * ports), F32),
            vmem((2, blocks, ports, size), F32),
        ]
        + [
            vmem((hist_n, blocks, share, size), BF16),
            vmem((hist_n - 1, blocks, share, size), BF16),
        ] * 2
        + [
            vmem((blocks + 4, share, size), BF16),
            vmem((blocks + 4, share, size), BF16),
            vmem((span, share, size), BF16),
            vmem((blocks, slots), jnp.int32),
            vmem((shells, blocks), jnp.int32),
            pltpu.SMEM((blocks, slots), jnp.int32),
            pltpu.SMEM((shells, blocks), jnp.int32),
            dma((shells, 2)), dma((shells, 2)),
            dma, dma,
            dma((2,)), dma((2,)),
            dma((blocks,)), dma((blocks,)),
            dma((hist_n - 1, 2)), dma((2,)),
            dma((2,)), dma((2,)),
            dma((hist_n - 1,)), dma((hist_n - 1,)),
            dma((hist_n - 1,)), dma((hist_n - 1,)),
            dma((2,)), dma((2,)), dma((2,)), dma((2,)), dma((2,)), dma((2,)),
            dma((shells,)), dma((shells,)), dma, dma, dma, dma((4,)),
        ],
        compiler_params=pltpu.CompilerParams(
            collective_id=0, has_side_effects=True, vmem_limit_bytes=64 * 1024 * 1024
        ),
    )(excitation, past, hist_tiles, hist_src, hist_count, near_tiles, hist_src, hist_count)
    return jnp.swapaxes(out, 2, 3)


def solution(mesh):
    return jax.shard_map(
        functools.partial(shards, mesh.shape["panel"], mesh.shape["hist"]),
        mesh=mesh,
        in_specs=(
            P(None, "panel", None, None),
            P("hist", "panel", None, None),
            P("hist", "panel", None, None, None),
            P("hist", "panel", None),
            P("hist", "panel"),
            P("panel", None, None, None),
        ),
        out_specs=P(None, "panel", None, "hist"),
        check_vma=False,
    )
```

```python
import functools

import jax
import jax.numpy as jnp
from jax import lax
from jax.experimental import pallas as pl
from jax.experimental.pallas import tpu as pltpu
from jax.sharding import PartitionSpec as P

WIN = 4
MESH = pl.DeviceIdType.MESH
F32 = jnp.float32
BF16 = jnp.bfloat16
NT = (((1,), (1,)), ((), ()))


def kernel(
    panels_n, hist_n,
    exc_ref, past_ref, tiles_ref, src_hbm, count_hbm, near_ref, src_ref, count_ref,
    out_ref,
    c0, c1, c2, c3, cprev, tv, t0, ne, exv, acc, drive, rs_out, rs_in, rs_out2, rs_in2,
    xe, xe2, cu, srcv, countv, srcs, counts,
    past_s, past_r, zown_s, zown_r, cp_s, cp_r, t0_s, t0_r, ix_s, ix_r, ne_s, ne_r,
    rs_s, rs_r, rs2_s, rs2_r, xe_s, xe_r, xe2_s, xe2_r, cu_s, cu_r,
    lpast, ltile, lnear, lexc, lt0, lix,
):
    cs = (c0, c1, c2, c3)
    shells, blocks, slots = tiles_ref.shape[:3]
    size = tiles_ref.shape[3]
    share = out_ref.shape[2]
    me = lax.axis_index("panel")
    zed = lax.axis_index("hist")
    has_l, has_r = me > 0, me < panels_n - 1
    has_d, has_u = zed > 0, zed < hist_n - 1
    none = blocks + 2 * WIN

    def when(condition, action):
        pl.when(condition)(action)

    local_past = [
        pltpu.make_async_copy(past_ref.at[k], cs[k].at[pl.ds(WIN, blocks)], lpast.at[k])
        for k in range(shells)
    ]
    local_tile = [
        pltpu.make_async_copy(tiles_ref.at[k], tv.at[k], ltile.at[k]) for k in range(shells)
    ]
    local_near = pltpu.make_async_copy(near_ref, ne.at[pl.ds(1, blocks)], lnear)
    local_exc = pltpu.make_async_copy(exc_ref, exv, lexc)
    local_t0 = pltpu.make_async_copy(tiles_ref.at[0], t0, lt0)
    local_ix = [
        pltpu.make_async_copy(src_hbm.at[0], srcv, lix.at[0]),
        pltpu.make_async_copy(count_hbm, countv, lix.at[1]),
    ]

    def pair(send, recv, out_right, in_left, out_left, in_right):
        right = pltpu.make_async_remote_copy(
            src_ref=out_right, dst_ref=in_left, send_sem=send.at[0], recv_sem=recv.at[0],
            device_id={"panel": jnp.minimum(me + 1, panels_n - 1)}, device_id_type=MESH,
        )
        left = pltpu.make_async_remote_copy(
            src_ref=out_left, dst_ref=in_right, send_sem=send.at[1], recv_sem=recv.at[1],
            device_id={"panel": jnp.maximum(me - 1, 0)}, device_id_type=MESH,
        )
        return right, left

    def pair_start(p):
        when(has_r, p[0].start)
        when(has_l, p[1].start)

    def pair_recv(p):
        when(has_l, p[0].wait_recv)
        when(has_r, p[1].wait_recv)

    def pair_send(p):
        when(has_r, p[0].wait_send)
        when(has_l, p[1].wait_send)

    low, high = pl.ds(0, WIN), pl.ds(WIN + blocks, WIN)
    first, last = pl.ds(WIN, WIN), pl.ds(blocks, WIN)
    past_pairs = [
        pair(
            past_s.at[k], past_r.at[k],
            past_ref.at[k, pl.ds(blocks - WIN, WIN)], cs[k].at[low],
            past_ref.at[k, pl.ds(0, WIN)], cs[k].at[high],
        )
        for k in range(shells)
    ]
    cp_pair = pair(cp_s, cp_r, cprev.at[last], cprev.at[low], cprev.at[first], cprev.at[high])
    near_pair = pair(
        ne_s, ne_r, near_ref.at[blocks - 1], ne.at[0], near_ref.at[0], ne.at[blocks + 1]
    )
    xe_out = (pl.ds(blocks, 2), pl.ds(0, 2), pl.ds(2, 2), pl.ds(blocks + 2, 2))
    xe_pair = pair(xe_s, xe_r, *[xe.at[w] for w in xe_out])
    xe2_pair = pair(xe2_s, xe2_r, *[xe2.at[w] for w in xe_out])
    cu_pair = pair(cu_s, cu_r, cu.at[last], cu.at[low], cu.at[first], cu.at[high])

    above = {"hist": jnp.minimum(zed + 1, hist_n - 1)}
    zown = pltpu.make_async_remote_copy(
        src_ref=past_ref.at[shells - 1], dst_ref=cprev.at[pl.ds(WIN, blocks)],
        send_sem=zown_s, recv_sem=zown_r, device_id=above, device_id_type=MESH,
    )

    def t0_copy(chunk, source):
        return pltpu.make_async_remote_copy(
            src_ref=source, dst_ref=t0.at[chunk], send_sem=t0_s.at[chunk],
            recv_sem=t0_r.at[chunk], device_id=above, device_id_type=MESH,
        )

    def t0_forward(chunk):
        def go():
            copy = t0_copy(chunk, t0.at[chunk])
            copy.wait_recv()
            copy.start()
        return go

    def t0_point(where):
        for chunk in range(blocks):
            if where == 1 + chunk:
                when((zed == 1) & has_u, t0_forward(chunk))
            if where == 3 + chunk:
                when((zed == 2) & has_u, t0_forward(chunk))
            if where == 6:
                when((zed > 2) & has_u, t0_forward(chunk))

    ix_copies = []
    for other in range(1, hist_n):
        ix_copies.append([
            pltpu.make_async_remote_copy(
                src_ref=source, dst_ref=target, send_sem=ix_s.at[other - 1, j],
                recv_sem=ix_r.at[j], device_id={"hist": other}, device_id_type=MESH,
            )
            for j, (source, target) in enumerate(((src_hbm.at[0], srcv), (count_hbm, countv)))
        ])

    def reduce_copies(send, recv, out, into):
        copies = []
        for step in range(1, hist_n):
            other = lax.rem(zed + step, hist_n)
            copies.append(pltpu.make_async_remote_copy(
                src_ref=out.at[other], dst_ref=into.at[step - 1],
                send_sem=send.at[step - 1], recv_sem=recv.at[step - 1],
                device_id={"hist": other}, device_id_type=MESH,
            ))
        return copies

    rs_copies = reduce_copies(rs_s, rs_r, rs_out, rs_in)
    rs2_copies = reduce_copies(rs2_s, rs2_r, rs_out2, rs_in2)

    for copy in local_past + [local_near, local_exc] + local_tile:
        copy.start()

    def at_zero():
        local_t0.start()
        for copy in local_ix:
            copy.start()
    when(zed == 0, at_zero)

    barrier = pltpu.get_barrier_semaphore()

    def greet(device):
        return lambda: pl.semaphore_signal(
            barrier, inc=1, device_id=device, device_id_type=MESH
        )
    when(has_r, greet({"panel": jnp.minimum(me + 1, panels_n - 1)}))
    when(has_l, greet({"panel": jnp.maximum(me - 1, 0)}))
    for step in range(1, hist_n):
        greet({"hist": lax.rem(zed + step, hist_n)})()
    for c in cs + (cprev,):
        c[none] = jnp.zeros((size, size), BF16)
    cu[none] = jnp.zeros((share, size), BF16)
    pl.semaphore_wait(
        barrier, hist_n - 1 + has_r.astype(jnp.int32) + has_l.astype(jnp.int32)
    )

    for p in past_pairs:
        pair_start(p)

    def spread():
        for copies in ix_copies:
            for copy in copies:
                copy.start()
        for chunk in range(blocks):
            t0_copy(chunk, tiles_ref.at[0, chunk]).start()
    when(zed == 0, spread)
    when(has_u, zown.start)

    local_exc.wait()
    for t in range(2):
        for n in range(blocks):
            drive[t, n] = exv[t, n].astype(F32).T
    local_near.wait()
    eye = lax.broadcasted_iota(jnp.int32, (size, size), 0) == lax.broadcasted_iota(
        jnp.int32, (size, size), 1
    )

    def diagonal(tile):
        return jnp.sum(jnp.where(eye, tile.astype(F32), 0.0), axis=0, keepdims=True)

    diag = {e: diagonal(ne[e, 1]) for e in range(1, blocks + 1)}

    def place(source, count, n, s):
        block = me * blocks + n + source
        live = (s < count) & (block >= 0) & (block < panels_n * blocks)
        return jnp.where(live, n + source + WIN, none)

    def tile_row(ref, n):
        return jnp.concatenate([ref[n, s] for s in range(slots)], axis=1)

    for k in range(shells):
        local_past[k].wait()
        local_tile[k].wait()
        pair_recv(past_pairs[k])
        if k == 2:
            pair_start(near_pair)
        for n in range(blocks):
            at = [place(src_ref[k, n, s], count_ref[k, n], n, s) for s in range(slots)]
            left = tile_row(tv.at[k], n)
            right = jnp.concatenate([cs[k][i] for i in at], axis=0)
            if k > 0:
                older = jnp.concatenate([cs[k - 1][i] for i in at], axis=0)
                right = jnp.concatenate([right, older], axis=1)
            part = jnp.dot(left, right, preferred_element_type=F32)
            if k == 0:
                acc[n, :, pl.ds(0, size)] = part
            elif k == 1:
                acc[n, :, pl.ds(0, size)] += part[:, :size]
                acc[n, :, pl.ds(size, size)] = part[:, size:]
            else:
                acc[n] += part
        t0_point(k)

    mine = pl.ds(pl.multiple_of(zed * share, share), share)

    for n in range(blocks):
        field = acc[n, :, pl.ds(0, size)].T
        drive[0, n] -= field
        rs_out[:, n] = field.reshape(hist_n, share, size).astype(BF16)
    for copy in rs_copies:
        copy.start()

    def pass_on():
        zown.wait_recv()
        pair_start(cp_pair)
    when(has_d, pass_on)
    t0_point(4)
    for copy in rs_copies:
        copy.wait_recv()

    def driven(t, n, into):
        g = drive[t, n, mine]
        for step in range(hist_n - 1):
            g = g - into[step, n].astype(F32)
        return g

    def begin(g, states, copy_pair):
        x = [g[n] / diag[n + 1] for n in range(blocks)]
        for n in range(blocks):
            states[n + 2] = x[n].astype(BF16)
        pair_start(copy_pair)
        return x

    g = [driven(0, n, rs_in) for n in range(blocks)]
    x = begin(g, xe, xe_pair)
    t0_point(5)

    def older_shell():
        pair_recv(cp_pair)
        for n in range(blocks):
            at = [place(src_ref[0, n, s], count_ref[0, n], n, s) for s in range(slots)]
            right = jnp.concatenate([cprev[i] for i in at], axis=0)
            acc[n, :, pl.ds(size, size)] += jnp.dot(
                tile_row(tv.at[0], n), right, preferred_element_type=F32
            )
    when(has_d, older_shell)
    for n in range(blocks):
        field = acc[n, :, pl.ds(size, size)].T
        drive[1, n] -= field
        rs_out2[:, n] = field.reshape(hist_n, share, size).astype(BF16)
    for copy in rs2_copies:
        copy.start()
    t0_point(6)
    pair_recv(near_pair)
    for e in (0, blocks + 1):
        diag[e] = diagonal(ne[e, 1])

    def applied(states, e):
        tiles = jnp.concatenate([ne[e, j] for j in range(3)], axis=1)
        return lax.dot_general(
            jnp.concatenate(states, axis=1), tiles, NT, preferred_element_type=F32
        )

    def sweeps(g, x, states, copy_pair):
        pair_recv(copy_pair)
        empty = jnp.zeros((share, size), BF16)
        held = [states[j] for j in range(blocks + 4)]
        for j in range(2):
            held[j] = jnp.where(has_l, held[j], empty)
            held[blocks + 2 + j] = jnp.where(has_r, held[blocks + 2 + j], empty)
        new = []
        for e in range(blocks + 2):
            by = applied(held[e : e + 3], e)
            if 0 < e <= blocks:
                x[e - 1] = x[e - 1] + (g[e - 1] - by) / diag[e]
                new.append(x[e - 1].astype(BF16))
            else:
                start = held[e + 1].astype(F32)
                value = (start + (start - by / diag[e])).astype(BF16)
                new.append(jnp.where(has_l if e == 0 else has_r, value, empty))
        return [
            (x[n] + (g[n] - applied(new[n : n + 3], n + 1)) / diag[n + 1]).astype(BF16)
            for n in range(blocks)
        ]

    now = sweeps(g, x, xe, xe_pair)
    for n in range(blocks):
        cu[WIN + n] = now[n]
    pair_start(cu_pair)
    for n in range(blocks):
        out_ref[0, n] = now[n]

    def here():
        local_t0.wait()
        for copy in local_ix:
            copy.wait()

    def there():
        for copy in ix_copies[0]:
            copy.wait_recv()

        def parts():
            for chunk in range(blocks):
                t0_copy(chunk, t0.at[chunk]).wait_recv()
        when(zed == hist_n - 1, parts)
    when(zed == 0, here)
    when(zed > 0, there)
    to_scalar = [
        pltpu.make_async_copy(srcv, srcs, lix.at[2]),
        pltpu.make_async_copy(countv, counts, lix.at[3]),
    ]
    for copy in to_scalar:
        copy.start()
    for copy in rs2_copies:
        copy.wait_recv()
    g = [driven(1, n, rs_in2) for n in range(blocks)]
    for copy in to_scalar:
        copy.wait()
    pair_recv(cu_pair)
    for n in range(blocks):
        at = [place(srcs[n, s], counts[0, n], n, s) for s in range(slots)]
        left = jnp.concatenate([cu[i] for i in at], axis=1)
        g[n] = g[n] - lax.dot_general(
            left, tile_row(t0, n), NT, preferred_element_type=F32
        )
    x = begin(g, xe2, xe2_pair)
    now = sweeps(g, x, xe2, xe2_pair)
    for n in range(blocks):
        out_ref[1, n] = now[n]

    for p in past_pairs + [near_pair, xe_pair, xe2_pair, cu_pair]:
        pair_send(p)
    when(has_d, lambda: pair_send(cp_pair))
    for copy in rs_copies + rs2_copies:
        copy.wait_send()
    when(has_u, zown.wait_send)

    def t0_sent():
        for chunk in range(blocks):
            t0_copy(chunk, t0.at[chunk]).wait_send()
    when(has_u, t0_sent)

    def ix_sent():
        for copies in ix_copies:
            for copy in copies:
                copy.wait_send()
    when(zed == 0, ix_sent)


def shards(panels_n, hist_n, excitation, past, hist_tiles, hist_src, hist_count, near_tiles):
    shells, blocks, slots, size = hist_tiles.shape[:4]
    ports = past.shape[3]
    share = ports // hist_n
    any_space = pl.BlockSpec(memory_space=pltpu.HBM)
    scalar = pl.BlockSpec(memory_space=pltpu.SMEM)
    span = blocks + 2 * WIN + 1
    dma = pltpu.SemaphoreType.DMA
    vmem = pltpu.VMEM
    out = pl.pallas_call(
        functools.partial(kernel, panels_n, hist_n),
        out_shape=jax.ShapeDtypeStruct((2, blocks, share, size), BF16),
        in_specs=[any_space] * 6 + [scalar] * 2,
        out_specs=pl.BlockSpec(memory_space=pltpu.VMEM),
        scratch_shapes=[vmem((span, size, ports), BF16)] * 5
        + [
            vmem((shells, blocks, slots, size, size), BF16),
            vmem((blocks, slots, size, size), BF16),
            vmem((blocks + 2, 3, size, size), BF16),
            vmem((2, blocks, size, ports), BF16),
            vmem((blocks, size, 2 * ports), F32),
            vmem((2, blocks, ports, size), F32),
        ]
        + [
            vmem((hist_n, blocks, share, size), BF16),
            vmem((hist_n - 1, blocks, share, size), BF16),
        ] * 2
        + [
            vmem((blocks + 4, share, size), BF16),
            vmem((blocks + 4, share, size), BF16),
            vmem((span, share, size), BF16),
            vmem((blocks, slots), jnp.int32),
            vmem((shells, blocks), jnp.int32),
            pltpu.SMEM((blocks, slots), jnp.int32),
            pltpu.SMEM((shells, blocks), jnp.int32),
            dma((shells, 2)), dma((shells, 2)),
            dma, dma,
            dma((2,)), dma((2,)),
            dma((blocks,)), dma((blocks,)),
            dma((hist_n - 1, 2)), dma((2,)),
            dma((2,)), dma((2,)),
            dma((hist_n - 1,)), dma((hist_n - 1,)),
            dma((hist_n - 1,)), dma((hist_n - 1,)),
            dma((2,)), dma((2,)), dma((2,)), dma((2,)), dma((2,)), dma((2,)),
            dma((shells,)), dma((shells,)), dma, dma, dma, dma((4,)),
        ],
        compiler_params=pltpu.CompilerParams(
            collective_id=0, has_side_effects=True, vmem_limit_bytes=64 * 1024 * 1024
        ),
    )(excitation, past, hist_tiles, hist_src, hist_count, near_tiles, hist_src, hist_count)
    return jnp.swapaxes(out, 2, 3)


def solution(mesh):
    return jax.shard_map(
        functools.partial(shards, mesh.shape["panel"], mesh.shape["hist"]),
        mesh=mesh,
        in_specs=(
            P(None, "panel", None, None),
            P("hist", "panel", None, None),
            P("hist", "panel", None, None, None),
            P("hist", "panel", None),
            P("hist", "panel"),
            P("panel", None, None, None),
        ),
        out_specs=P(None, "panel", None, "hist"),
        check_vma=False,
    )
```
